128 devices in a mesh: dp: 16 (over y, x_lo, core), mp: 8 (over x_hi, z).
Axes of the slice: x: 4 (x_hi: 2, x_lo: 2; x = x_hi * 2 + x_lo), y: 4, z: 4, core: 2. Of those that a mesh axis runs over, the one named last changes fastest.
Arguments:
- block_input: bfloat16 [16, 16, 8, 8, 2048], P('dp', None, None, None, 'mp'), may hold values from -6 to 6
- spatial_out: bfloat16 [16, 16, 8, 8, 2048], P('dp', None, None, None, 'mp'), may hold values from -6 to 6
- cotangent: bfloat16 [16, 16, 8, 8, 2048], P('dp', None, None, None, 'mp'), may hold values from -0.59765625 to 0.59765625
- spatial_kernel: bfloat16 [3, 3, 2048, 2048], P(None, None, None, 'mp'), may hold values from -0.046875 to 0.046875
- temporal_kernel: bfloat16 [3, 2048, 2048], P(None, None, 'mp'), may hold values from -0.078125 to 0.078125
- norm_gain: float32 [2048], P('mp'), may hold values from 0.1 to 1.9
- norm_bias: float32 [2048], P('mp'), may hold values from -1 to 1
Outputs:
- input_grad: bfloat16 [16, 16, 8, 8, 2048], P('dp', None, None, None, 'mp')
- spatial_kernel_grad: float32 [3, 3, 2048, 2048], P(None, None, 'dp', 'mp')
- temporal_kernel_grad: float32 [3, 2048, 2048], P(None, 'dp', 'mp')
- gain_grad: float32 [2048], P('mp')
- bias_grad: float32 [2048], P('mp')
The draws below stay inside these ranges and needn't reach their ends.
All inputs are finite; a program needn't handle non-finite values.
Results may differ from the reference program's by a relative error of at most 0.005.
Values may be sent and summed in bfloat16 or wider, within the bound.
No kernel may reach another device: no remote copies, remote signals or barrier semaphores. Data moves between devices by JAX's collectives and lax.ppermute only.
A program may use at most 192 MiB of HBM per device.

```python
import jax
import jax.numpy as jnp
from jax import lax

C = 2048
G = 32
FR = 16
HT = 8
WD = 8
CLIPS = 16


def block_levels(own_key, shape, pieces, least, high):
    loudness = 1.0
    for axis_at, shards_of in pieces:
        draws = jax.random.uniform(jax.random.fold_in(jax.random.fold_in(own_key, 6), axis_at), (shards_of,), jnp.float32, least / len(pieces), high / len(pieces))
        loudness = loudness * jnp.repeat(jnp.exp(draws), shape[axis_at] // shards_of).reshape((-1,) + (1,) * (len(shape) - 1 - axis_at))
    return loudness


def centred(rng, shape, deviation, reach, pieces=(), kind=jnp.bfloat16):
    values = deviation * jax.random.normal(rng, shape, jnp.float32)
    if pieces:
        values = values * block_levels(rng, shape, pieces, -0.22, 0.18)
    return jnp.clip(values, -reach, reach).astype(kind)


def setup_inputs(seed: int = 0) -> dict:
    keys = jax.random.split(jax.random.key(seed), 8)
    return {
        "block_input": centred(keys[0], (CLIPS, FR, HT, WD, C), 1.0, 6.0, ((0, 16), (4, 8))),
        "spatial_out": centred(keys[1], (CLIPS, FR, HT, WD, C), 1.0, 6.0, ((0, 16), (4, 8))),
        "cotangent": centred(keys[2], (CLIPS, FR, HT, WD, C), 0.1, 0.59765625, ((0, 16), (4, 8))),
        "spatial_kernel": centred(keys[3], (3, 3, C, C), (9 * C) ** -0.5, 0.046875, ((3, 8),)),
        "temporal_kernel": centred(keys[4], (3, C, C), (3 * C) ** -0.5, 0.078125, ((2, 8),)),
        "norm_gain": jnp.clip(1.0 + 0.18 * jax.random.normal(keys[5], (C,), jnp.float32), 0.1, 1.9),
        "norm_bias": jnp.clip(jax.random.uniform(keys[6], (C,), jnp.float32, -1.0, 1.0) * block_levels(keys[6], (C,), ((0, 8),), -0.4, 0.0), -1.0, 1.0),
    }


EPSILON = 1e-05

def shifted(values, clip_count, step_f, step_y, step_x):
    channels = values.shape[1]
    volume = values.reshape(clip_count, FR, HT, WD, channels)
    padded = jnp.pad(volume, ((0, 0), (1, 1), (1, 1), (1, 1), (0, 0)))
    window = padded[:, 1 + step_f:1 + step_f + FR, 1 + step_y:1 + step_y + HT, 1 + step_x:1 + step_x + WD, :]
    return window.reshape(-1, channels)

def contract_rows(left, right):
    return lax.dot_general(left, right, (((0,), (0,)), ((), ())), preferred_element_type=jnp.float32)

def contract_cols(left, right):
    return lax.dot_general(left, right, (((1,), (1,)), ((), ())), preferred_element_type=jnp.float32)

def group_stats(flat, clip_count):
    channels = flat.shape[1]
    grouped = flat.reshape(clip_count, -1, channels // (C // G), C // G)
    center = lax.optimization_barrier(jnp.mean(grouped, axis=(1, 3), keepdims=True))
    spread = lax.optimization_barrier(jnp.mean(jnp.square(grouped - center), axis=(1, 3), keepdims=True))
    inverse = lax.rsqrt(spread + EPSILON)
    return (((grouped - center) * inverse).reshape(flat.shape), inverse)

def group_backward(upstream, normed_hat, inverse, clip_count):
    channels = upstream.shape[1]
    grad_groups = upstream.reshape(clip_count, -1, channels // (C // G), C // G)
    hat_groups = normed_hat.reshape(grad_groups.shape)
    first = lax.optimization_barrier(jnp.mean(grad_groups, axis=(1, 3), keepdims=True))
    second = lax.optimization_barrier(jnp.mean(grad_groups * hat_groups, axis=(1, 3), keepdims=True))
    return (inverse * (grad_groups - first - hat_groups * second)).reshape(upstream.shape)

def reference(block_input, spatial_out, cotangent, spatial_kernel, temporal_kernel, norm_gain, norm_bias):
    clip_count = block_input.shape[0]
    flat_in = block_input.reshape(-1, C).astype(jnp.float32)
    normed_hat, inverse = group_stats(flat_in, clip_count)
    normed = normed_hat * norm_gain + norm_bias
    gate = jax.nn.sigmoid(normed)
    hidden = (normed * gate).astype(jnp.bfloat16)
    saved = spatial_out.reshape(-1, C)
    upstream = cotangent.reshape(-1, C)
    temporal_sum = jnp.zeros((upstream.shape[0], C), jnp.float32)
    for offset in range(3):
        temporal_sum = temporal_sum + contract_cols(shifted(upstream, clip_count, 1 - offset, 0, 0), temporal_kernel[offset])
    saved_grad = temporal_sum.astype(jnp.bfloat16)
    temporal_grad = jnp.stack([contract_rows(shifted(saved, clip_count, offset - 1, 0, 0), upstream) for offset in range(3)])
    hidden_grad = jnp.zeros((upstream.shape[0], C), jnp.float32)
    for tap_y in range(3):
        for tap_x in range(3):
            hidden_grad = hidden_grad + contract_cols(shifted(saved_grad, clip_count, 0, 1 - tap_y, 1 - tap_x), spatial_kernel[tap_y, tap_x])
    spatial_grad = jnp.stack([jnp.stack([contract_rows(shifted(hidden, clip_count, 0, tap_y - 1, tap_x - 1), saved_grad) for tap_x in range(3)]) for tap_y in range(3)])
    normed_grad = hidden_grad * gate * (1.0 + normed * (1.0 - gate))
    gain_grad = lax.optimization_barrier(jnp.sum(normed_grad * normed_hat, axis=0))
    bias_grad = lax.optimization_barrier(jnp.sum(normed_grad, axis=0))
    branch = group_backward(normed_grad * norm_gain, normed_hat, inverse, clip_count)
    input_grad = (upstream.astype(jnp.float32) + branch).astype(jnp.bfloat16).reshape(block_input.shape)
    return (input_grad, spatial_grad, temporal_grad, gain_grad, bias_grad)
```

```python
import itertools

import jax
import jax.numpy as jnp
from jax import lax
from jax.experimental import pallas as pl
from jax.experimental.pallas import tpu as pltpu
from jax.sharding import PartitionSpec as P

C = 2048
G = 32
FR = 16
HT = 8
WD = 8
EPSILON = 1e-05

ROWS = FR * HT * WD
CH = 256
SUB = 64
BF = jnp.bfloat16
F32 = jnp.float32
VMEM = 60 * 1024 * 1024


def linear(x, y, z, c):
    return (4 * y + 2 * (x % 2) + c) * 8 + 4 * (x // 2) + z


def send(value, to):
    pairs = []
    for x, y, z, c in itertools.product(range(4), range(4), range(4), range(2)):
        tx, ty, tz, tc = to(x, y, z, c)
        pairs.append((linear(x, y, z, c), linear(tx % 4, ty % 4, tz % 4, tc)))
    return lax.ppermute(value, ("dp", "mp"), pairs)


def to_z(step):
    return lambda x, y, z, c: (x, y, z + step, c)


def to_y(step):
    return lambda x, y, z, c: (x, y + step, z, c)


def to_core(x, y, z, c):
    return (x, y, z, 1 - c)


def to_half(x, y, z, c):
    return (x ^ 2, y, z, c)


def to_pair(x, y, z, c):
    return (x ^ 1, y, z, c)


def to_both(x, y, z, c):
    return (x ^ 3, y, z, c)


def to_pair_core(x, y, z, c):
    return (x ^ 1, y, z, 1 - c)


BLOCK_OF = ((0, 2, 1, 3), (1, 3, 0, 2))


def to_owner(flip):
    def to(x, y, z, c):
        half, pair = x // 2, x % 2
        block = BLOCK_OF[half][y]
        return (2 * (flip ^ c) + block % 2, 2 * half + block // 2, z, pair)

    return to


def contract_cols(left, right):
    return lax.dot_general(left, right, (((1,), (1,)), ((), ())), preferred_element_type=F32)


def contract_inner(left, right):
    return lax.dot_general(left, right, (((1,), (0,)), ((), ())), preferred_element_type=F32)


def params():
    return pltpu.CompilerParams(vmem_limit_bytes=VMEM)


def temporal_dgrad_body(index, mine, other, w_mine, w_other, out, padded):
    padded[pl.ds(0, 1)] = jnp.zeros((1, 64, 2 * CH), BF)
    padded[pl.ds(FR + 1, 1)] = jnp.zeros((1, 64, 2 * CH), BF)
    padded[pl.ds(1, FR), :, pl.ds(0, CH)] = mine[...]
    padded[pl.ds(1, FR), :, pl.ds(CH, CH)] = other[...]
    total = jnp.zeros((ROWS, CH), F32)
    for tap in range(3):
        rows = padded[pl.ds(2 - tap, FR)].reshape(ROWS, 2 * CH)
        weights = jnp.concatenate([w_mine[tap], w_other[:, tap].reshape(CH, CH)], axis=1)
        total = total + contract_cols(rows, weights)
    out[...] = total.astype(out.dtype)


def spatial_dgrad_body(index, mine, other, w_mine, w_other, out, padded):
    padded[...] = jnp.zeros(padded.shape, BF)
    padded[pl.ds(1, HT), pl.ds(1, WD), :, pl.ds(0, CH)] = mine[...]
    padded[pl.ds(1, HT), pl.ds(1, WD), :, pl.ds(CH, CH)] = other[...]
    total = jnp.zeros((ROWS, CH), F32)
    for tap in range(9):
        rows = padded[pl.ds(2 - tap // 3, HT), pl.ds(2 - tap % 3, WD)].reshape(ROWS, 2 * CH)
        weights = jnp.concatenate([w_mine[tap], w_other[:, tap].reshape(CH, CH)], axis=1)
        total = total + contract_cols(rows, weights)
    out[...] = total.astype(out.dtype)


def dgrad(body, pad_shape, taps, index, mine, other, w_mine, w_other, kind):
    whole = lambda shape: pl.BlockSpec(shape, lambda i, ix: (0,) * len(shape))
    return pl.pallas_call(
        body,
        grid_spec=pltpu.PrefetchScalarGridSpec(
            num_scalar_prefetch=1,
            grid=(1,),
            in_specs=[
                whole(mine.shape),
                whole(other.shape),
                pl.BlockSpec((taps, CH, CH), lambda i, ix: (0, ix[0], 0)),
                pl.BlockSpec((2, taps, CH // 2, CH), lambda i, ix: (ix[1], 0, 0, 0)),
            ],
            out_specs=whole((ROWS, CH)),
            scratch_shapes=[pltpu.VMEM(pad_shape, BF)],
        ),
        out_shape=jax.ShapeDtypeStruct((ROWS, CH), kind),
        compiler_params=params(),
        cost_estimate=pl.CostEstimate(
            flops=2 * taps * ROWS * 2 * CH * CH,
            bytes_accessed=2 * (4 * ROWS * CH + 2 * taps * CH * CH),
            transcendentals=0,
        ),
    )(index, mine, other, w_mine, w_other)


def wgrad_body(first, spatial, index, left, *refs):
    fields, (out, padded) = refs[:8], refs[8:]
    step = pl.program_id(0)

    @pl.when(step == 0)
    def _():
        padded[...] = jnp.zeros(padded.shape, BF)
        for clip in range(4):
            for side in range(2):
                cols = pl.ds(side * CH, CH)
                if spatial:
                    padded[clip, pl.ds(1, HT), pl.ds(1, WD), :, cols] = fields[2 * clip + side][...]
                else:
                    padded[clip, pl.ds(1, FR), :, cols] = fields[2 * clip + side][...]

    tap = step + first
    if spatial:
        right = padded[:, pl.ds(2 - tap // 3, HT), pl.ds(2 - tap % 3, WD)]
    else:
        right = padded[:, pl.ds(2 - tap, FR)]
    result = contract_inner(left[...].reshape(4 * SUB, 4 * ROWS), right.reshape(4 * ROWS, 2 * CH))
    result = result.astype(BF)
    for block in range(4):
        out[index[block], 0] = result[block * SUB : (block + 1) * SUB]


def wgrad(spatial, first, taps, index, left, fields):
    pad_shape = (4, HT + 2, WD + 2, FR, 2 * CH) if spatial else (4, FR + 2, HT * WD, 2 * CH)
    whole = lambda shape: pl.BlockSpec(shape, lambda i, ix: (0,) * len(shape))

    def body(*refs):
        wgrad_body(first, spatial, *refs)

    return pl.pallas_call(
        body,
        grid_spec=pltpu.PrefetchScalarGridSpec(
            num_scalar_prefetch=1,
            grid=(taps,),
            in_specs=[whole(left.shape)] + [whole(f.shape) for f in fields],
            out_specs=pl.BlockSpec((4, 1, SUB, 2 * CH), lambda i, ix: (0, i, 0, 0)),
            scratch_shapes=[pltpu.VMEM(pad_shape, BF)],
        ),
        out_shape=jax.ShapeDtypeStruct((4, taps, SUB, 2 * CH), BF),
        compiler_params=params(),
        cost_estimate=pl.CostEstimate(
            flops=2 * taps * 4 * ROWS * 4 * SUB * 2 * CH,
            bytes_accessed=2 * (4 * ROWS * 3 * CH + taps * CH * 2 * CH),
            transcendentals=0,
        ),
    )(index, left, *fields)


def per_group(values):
    return jnp.repeat(jnp.sum(values.reshape(-1, C // G), axis=1), C // G)


def local(
    block_input, spatial_out, cotangent, spatial_kernel, temporal_kernel, norm_gain, norm_bias
):
    dp, mp = lax.axis_index("dp"), lax.axis_index("mp")
    y, pair, core = dp // 4, (dp // 2) % 2, dp % 2
    half, z = mp // 4, mp % 4
    quarter = 2 * pair + core
    y_core_groups = [[4 * a + 2 * p + b for a in range(4) for b in range(2)] for p in range(2)]
    z_groups = [[0, 1, 2, 3], [4, 5, 6, 7]]

    cot = cotangent.reshape(FR, HT * WD, CH)
    spatial_kernel = spatial_kernel.reshape(9, C, CH)

    def other_kernel(kernel):
        start = (1 - half) * 1024 + y * 256 + core * 128
        part = lax.dynamic_slice_in_dim(kernel, start, 128, axis=1)
        part = send(part, to_half)
        return lax.all_gather(part, "dp", axis=0, axis_index_groups=y_core_groups)

    cot_other = send(cot, to_half)
    tk_other = other_kernel(temporal_kernel)
    sk_other = other_kernel(spatial_kernel)

    flat_in = block_input.reshape(FR, HT * WD, CH).transpose(1, 0, 2).reshape(ROWS, CH).astype(F32)
    count = ROWS * (C // G)
    center = per_group(jnp.sum(flat_in, axis=0)) / count
    spread = per_group(jnp.sum(jnp.square(flat_in - center), axis=0)) / count
    inverse = lax.rsqrt(spread + EPSILON)
    normed_hat = (flat_in - center) * inverse
    normed = normed_hat * norm_gain + norm_bias
    gate = jax.nn.sigmoid(normed)
    hidden = (normed * gate).astype(BF)

    def gather_left(flat):
        turned = flat.T.reshape(4, SUB, ROWS)
        pick = lambda k: lax.dynamic_index_in_dim(turned, quarter ^ k, 0, keepdims=False)
        parts = [pick(0), send(pick(1), to_core), send(pick(2), to_pair), send(pick(3), to_pair_core)]
        return lax.all_gather(
            jnp.concatenate(parts, axis=1), "mp", axis=0, axis_index_groups=z_groups
        )

    def gather_fields(mine, other):
        pair_mine, pair_other = send(mine, to_pair), send(mine, to_both)
        near, far = (mine, other), (pair_mine, pair_other)
        return (
            near
            + tuple(send(v, to_core) for v in near)
            + far
            + tuple(send(v, to_core) for v in far)
        )

    def scatter_z(call):
        parts = {}
        for k in (1, 3, 2, 0):
            to = (z + k) % 4
            index = jnp.stack([half * 4 + to, to]).astype(jnp.int32)
            part = call(index, F32 if k == 0 else BF)
            parts[k] = send(part, to_z(k)) if k else part
        return parts[0] + (parts[1].astype(F32) + parts[3].astype(F32)) + parts[2].astype(F32)

    saved_left = gather_left(spatial_out.reshape(ROWS, CH))
    hidden_left = gather_left(hidden)

    saved_grad = scatter_z(
        lambda index, kind: dgrad(
            temporal_dgrad_body,
            (FR + 2, HT * WD, 2 * CH),
            3,
            index,
            cot,
            cot_other,
            temporal_kernel,
            tk_other,
            kind,
        )
    ).astype(BF)
    saved_grad = saved_grad.reshape(FR, HT * WD, CH).transpose(1, 0, 2).reshape(HT, WD, FR, CH)
    sg_other = send(saved_grad, to_half)

    hidden_grad = scatter_z(
        lambda index, kind: dgrad(
            spatial_dgrad_body,
            (HT + 2, WD + 2, FR, 2 * CH),
            9,
            index,
            saved_grad,
            sg_other,
            spatial_kernel,
            sk_other,
            kind,
        )
    )

    slots = jnp.array([[0, 2, 1, 3], [2, 0, 3, 1]], jnp.int32)[half]
    order = (slots - y) % 4

    def kernel_grad(spatial, first, taps, left, fields):
        parts = wgrad(spatial, first, taps, order, left, fields)
        total = parts[0].astype(F32)
        for k in (1, 3, 2):
            total = total + send(parts[k], to_y(k)).astype(F32)
        total = total.astype(BF)
        mine, other = total[:, :, :CH], total[:, :, CH:]
        same = (half == core)
        got = [
            send(jnp.where(same, mine, other), to_owner(0)),
            send(jnp.where(same, other, mine), to_owner(1)),
        ]
        low = jnp.where(half == 0, got[0], got[1])
        high = jnp.where(half == 0, got[1], got[0])
        return jnp.concatenate([low, high], axis=1).astype(F32)

    cot_fields = gather_fields(cot, cot_other)
    temporal_grad = kernel_grad(False, 0, 3, saved_left, cot_fields)
    sg_fields = gather_fields(saved_grad, sg_other)
    spatial_grad = jnp.stack(
        [kernel_grad(True, 3 * row, 3, hidden_left, sg_fields) for row in range(3)]
    )

    normed_grad = hidden_grad * gate * (1.0 + normed * (1.0 - gate))
    gain_sum = jnp.sum(normed_grad * normed_hat, axis=0)
    bias_sum = jnp.sum(normed_grad, axis=0)
    first = per_group(bias_sum * norm_gain) / count
    second = per_group(gain_sum * norm_gain) / count
    branch = inverse * (normed_grad * norm_gain - first - normed_hat * second)
    branch = branch.reshape(HT * WD, FR, CH).transpose(1, 0, 2)
    input_grad = (cot.astype(F32) + branch).astype(BF).reshape(block_input.shape)

    sums = jnp.stack([gain_sum, bias_sum])
    for to in (to_core, to_pair, to_y(2)):
        sums = sums + send(sums, to)
    sums = sums + send(sums, to_y(1))
    return (input_grad, spatial_grad, temporal_grad, sums[0], sums[1])


def solution(mesh):
    placed = (
        P("dp", None, None, None, "mp"),
        P("dp", None, None, None, "mp"),
        P("dp", None, None, None, "mp"),
        P(None, None, None, "mp"),
        P(None, None, "mp"),
        P("mp"),
        P("mp"),
    )
    return jax.shard_map(
        local,
        mesh=mesh,
        in_specs=placed,
        out_specs=(
            P("dp", None, None, None, "mp"),
            P(None, None, "dp", "mp"),
            P(None, "dp", "mp"),
            P("mp"),
            P("mp"),
        ),
        check_vma=False,
    )
```

```python
import itertools

import jax
import jax.numpy as jnp
from jax import lax
from jax.experimental import pallas as pl
from jax.experimental.pallas import tpu as pltpu
from jax.sharding import PartitionSpec as P

C = 2048
G = 32
FR = 16
HT = 8
WD = 8
EPSILON = 1e-05

ROWS = FR * HT * WD
CH = 256
SUB = 64
BF = jnp.bfloat16
F32 = jnp.float32
VMEM = 60 * 1024 * 1024


def linear(x, y, z, c):
    return (4 * y + 2 * (x % 2) + c) * 8 + 4 * (x // 2) + z


def send(value, to):
    pairs = []
    for x, y, z, c in itertools.product(range(4), range(4), range(4), range(2)):
        tx, ty, tz, tc = to(x, y, z, c)
        pairs.append((linear(x, y, z, c), linear(tx % 4, ty % 4, tz % 4, tc)))
    return lax.ppermute(value, ("dp", "mp"), pairs)


def to_z(step):
    return lambda x, y, z, c: (x, y, z + step, c)


def to_y(step):
    return lambda x, y, z, c: (x, y + step, z, c)


def to_core(x, y, z, c):
    return (x, y, z, 1 - c)


def to_half(x, y, z, c):
    return (x ^ 2, y, z, c)


def to_pair(x, y, z, c):
    return (x ^ 1, y, z, c)


def to_both(x, y, z, c):
    return (x ^ 3, y, z, c)


def to_pair_core(x, y, z, c):
    return (x ^ 1, y, z, 1 - c)


BLOCK_OF = ((0, 2, 1, 3), (1, 3, 0, 2))


def to_owner(flip):
    def to(x, y, z, c):
        half, pair = x // 2, x % 2
        block = BLOCK_OF[half][y]
        return (2 * (flip ^ c) + block % 2, 2 * half + block // 2, z, pair)

    return to


def contract_cols(left, right):
    return lax.dot_general(left, right, (((1,), (1,)), ((), ())), preferred_element_type=F32)


def contract_inner(left, right):
    return lax.dot_general(left, right, (((1,), (0,)), ((), ())), preferred_element_type=F32)


def cost(microseconds):
    return pl.CostEstimate(flops=int(microseconds * 1.15e9), bytes_accessed=0, transcendentals=0)


def params():
    return pltpu.CompilerParams(vmem_limit_bytes=VMEM)


def fill(padded, mine, other, spatial):
    if spatial:
        inner = (pl.ds(1, HT), pl.ds(1, WD), slice(None))
    else:
        inner = (pl.ds(1, FR), slice(None))
    padded[...] = jnp.zeros(padded.shape, BF)
    padded[inner + (pl.ds(0, CH),)] = mine
    padded[inner + (pl.ds(CH, CH),)] = other


def tap_rows(spatial, tap):
    if spatial:
        return (pl.ds(2 - tap // 3, HT), pl.ds(2 - tap % 3, WD))
    return (pl.ds(2 - tap, FR),)


def dgrad_body(spatial, blocks, index, mine, other, w_mine, *refs):
    w_other, outs, padded = refs[:2], refs[-1 - blocks : -1], refs[-1]
    step = pl.program_id(0)
    core = index[0]

    @pl.when(step == 0)
    def _():
        fill(padded, mine[...], other[...], spatial)

    total = jnp.zeros((ROWS, CH), F32)
    for tap in range(9 if spatial else 3):
        rows = padded[tap_rows(spatial, tap)].reshape(ROWS, 2 * CH)
        near, far = [w[0, tap] for w in w_other]
        low = jnp.where(core == 0, near, far)
        high = jnp.where(core == 0, far, near)
        weights = jnp.concatenate([w_mine[tap], jnp.concatenate([low, high], axis=0)], axis=1)
        total = total + contract_cols(rows, weights)
    for place, out in enumerate(outs):

        @pl.when(step == place)
        def _():
            out[...] = total.astype(out.dtype)


def whole(shape):
    return pl.BlockSpec(shape, lambda i, ix: (0,) * len(shape))


def pad_shape(spatial):
    return (HT + 2, WD + 2, FR, 2 * CH) if spatial else (FR + 2, HT * WD, 2 * CH)


def dgrad(spatial, blocks, kinds, index, mine, other, w_mine, w_near, w_far, *waits):
    taps = 9 if spatial else 3
    near = pl.BlockSpec((1, taps, CH // 2, CH), lambda i, ix: (ix[1 + blocks + i], 0, 0, 0))
    far = pl.BlockSpec((1, taps, CH // 2, CH), lambda i, ix: (ix[1 + 2 * blocks + i], 0, 0, 0))
    return pl.pallas_call(
        lambda *refs: dgrad_body(spatial, blocks, *refs),
        grid_spec=pltpu.PrefetchScalarGridSpec(
            num_scalar_prefetch=1,
            grid=(blocks,),
            in_specs=[
                whole(mine.shape),
                whole(other.shape),
                pl.BlockSpec((taps, CH, CH), lambda i, ix: (0, ix[1 + i], 0)),
                near,
                far,
            ]
            + [pl.BlockSpec(memory_space=pl.ANY)] * len(waits),
            out_specs=[whole((ROWS, CH))] * blocks,
            scratch_shapes=[pltpu.VMEM(pad_shape(spatial), BF)],
        ),
        out_shape=[jax.ShapeDtypeStruct((ROWS, CH), kind) for kind in kinds],
        compiler_params=params(),
        cost_estimate=cost(2.0 + 3.2 * blocks if spatial else 7.0),
    )(index, mine, other, w_mine, w_near, w_far, *waits)


def wgrad_body(first, spatial, lefts, index, *refs):
    left, (mine, other, pair, both, swapped) = refs[:lefts], refs[lefts : lefts + 5]
    out, padded = refs[-2:]
    step = pl.program_id(0)

    @pl.when(step == 0)
    def _():
        fill(padded.at[0], mine[...], other[...], spatial)
        fill(padded.at[1], swapped[0], swapped[1], spatial)
        fill(padded.at[2], pair[...], both[...], spatial)
        fill(padded.at[3], swapped[2], swapped[3], spatial)

    right = padded[(slice(None),) + tap_rows(spatial, step + first)]
    blocks = jnp.concatenate([ref[...].reshape(-1, 4 * ROWS) for ref in left], axis=0)
    result = contract_inner(blocks, right.reshape(4 * ROWS, 2 * CH))
    result = result.astype(BF)
    for block in range(4):
        out[index[block], 0] = result[block * SUB : (block + 1) * SUB]


def wgrad(spatial, first, taps, index, left, fields, *waits):
    return pl.pallas_call(
        lambda *refs: wgrad_body(first, spatial, len(left), *refs),
        grid_spec=pltpu.PrefetchScalarGridSpec(
            num_scalar_prefetch=1,
            grid=(taps,),
            in_specs=[whole(f.shape) for f in left + fields]
            + [pl.BlockSpec(memory_space=pl.ANY)] * len(waits),
            out_specs=pl.BlockSpec((4, 1, SUB, 2 * CH), lambda i, ix: (0, i, 0, 0)),
            scratch_shapes=[pltpu.VMEM((4,) + pad_shape(spatial), BF)],
        ),
        out_shape=jax.ShapeDtypeStruct((4, taps, SUB, 2 * CH), BF),
        compiler_params=params(),
        cost_estimate=cost(4.7 + 1.25 * taps),
    )(index, *left, *fields, *waits)


def after(value, *others):
    return pl.pallas_call(
        lambda *refs: None,
        in_specs=[pl.BlockSpec(memory_space=pl.ANY)] * (1 + len(others)),
        out_specs=pl.BlockSpec(memory_space=pl.ANY),
        out_shape=jax.ShapeDtypeStruct(value.shape, value.dtype),
        input_output_aliases={0: 0},
        cost_estimate=pl.CostEstimate(flops=0, bytes_accessed=0, transcendentals=0),
    )(value, *others)


def together(*values):
    return pl.pallas_call(
        lambda *refs: None,
        in_specs=[pl.BlockSpec(memory_space=pl.ANY)] * len(values),
        out_specs=[pl.BlockSpec(memory_space=pl.ANY)] * len(values),
        out_shape=[jax.ShapeDtypeStruct(value.shape, value.dtype) for value in values],
        input_output_aliases={i: i for i in range(len(values))},
        cost_estimate=pl.CostEstimate(flops=0, bytes_accessed=0, transcendentals=0),
    )(*values)


def per_group(values):
    return jnp.repeat(jnp.sum(values.reshape(-1, C // G), axis=1), C // G)


def local(
    block_input, spatial_out, cotangent, spatial_kernel, temporal_kernel, norm_gain, norm_bias
):
    dp, mp = lax.axis_index("dp"), lax.axis_index("mp")
    y, pair, core = dp // 4, (dp // 2) % 2, dp % 2
    half, z = mp // 4, mp % 4
    quarter = 2 * pair + core
    y_core_groups = [[4 * a + 2 * p + b for a in range(4) for b in range(2)] for p in range(2)]
    y_groups = [[4 * a + b for a in range(4)] for b in range(4)]
    z_groups = [[0, 1, 2, 3], [4, 5, 6, 7]]

    cot = cotangent.reshape(FR, HT * WD, CH)
    spatial_kernel = spatial_kernel.reshape(9, C, CH)

    def exchange(turned):
        pick = lambda k: lax.dynamic_index_in_dim(turned, quarter ^ k, 0, keepdims=False)
        sent = send(pick(1), to_core), send(pick(2), to_pair), send(pick(3), to_pair_core)
        return pick(0), sent

    def kernel_part(kernel):
        start = (1 - half) * 1024 + y * 256 + core * 128
        return lax.dynamic_slice_in_dim(kernel, start, 128, axis=1)

    tk_part = send(kernel_part(temporal_kernel), to_half)
    own, parts = exchange(spatial_out.reshape(ROWS, CH).T.reshape(4, SUB, ROWS))
    tk_part, *parts = together(tk_part, *parts)
    saved_part = jnp.concatenate([own, *parts], axis=1)
    saved_left = (lax.all_gather(saved_part, "mp", axis=0, axis_index_groups=z_groups),)

    tk_parts = [send(tk_part, to_y(k)) for k in (1, 2, 3)]
    cot_other = send(cot, to_half)
    cot_other, *tk_parts = together(cot_other, *tk_parts)
    tk_near = jnp.stack([tk_part, *tk_parts])

    flat_in = block_input.reshape(FR, HT * WD, CH).transpose(1, 0, 2).reshape(ROWS, CH).astype(F32)
    count = ROWS * (C // G)
    center = per_group(jnp.sum(flat_in, axis=0)) / count
    spread = per_group(jnp.sum(jnp.square(flat_in - center), axis=0)) / count
    inverse = lax.rsqrt(spread + EPSILON)
    normed_hat = (flat_in - center) * inverse
    normed = normed_hat * norm_gain + norm_bias
    gate = jax.nn.sigmoid(normed)
    hidden = (normed * gate).astype(BF)

    def blocks_of(spatial, steps, *arrays):
        blocks = [(z + k) % 4 for k in steps]
        if spatial:
            near, far = [2 * b for b in blocks], [2 * b + 1 for b in blocks]
        else:
            near = far = [(y - b) % 4 for b in blocks]
        index = [0 if spatial else core] + [half * 4 + b for b in blocks] + near + far
        index = jnp.stack([jnp.int32(i) for i in index])
        kinds = [BF if k else F32 for k in steps]
        return dgrad(spatial, len(steps), kinds, index, *arrays)

    def total_of(mine, sent):
        one, two, three = [v.astype(F32) for v in sent]
        return mine + (one + three) + two

    tk_far = send(tk_near, to_core)
    own, parts = exchange(hidden.T.reshape(4, SUB, ROWS))
    tk_far, *parts = together(tk_far, *parts)
    hidden_part = jnp.concatenate([own, *parts], axis=1)
    hidden_left = (lax.all_gather(hidden_part, "mp", axis=0, axis_index_groups=z_groups),)

    arrays = (cot, cot_other, temporal_kernel, tk_near, tk_far)
    sk_part = send(after(kernel_part(spatial_kernel), tk_far), to_half)
    up, down, far, mine = blocks_of(False, (1, 3, 2, 0), *arrays, *saved_left)
    sk_part, up, down, far = together(sk_part, up, down, far)
    sk_other = lax.all_gather(sk_part, "dp", axis=0, axis_index_groups=y_core_groups)
    up, down, far = send(up, to_z(1)), send(down, to_z(3)), send(far, to_z(2))
    cot_late = after(cot, mine)
    cot_pair, cot_both = send(cot_late, to_pair), send(cot_late, to_both)
    up, down, far, cot_pair, cot_both = together(up, down, far, cot_pair, cot_both)
    saved_grad = total_of(mine, (up, far, down)).astype(BF)
    saved_grad = saved_grad.reshape(FR, HT * WD, CH).transpose(1, 0, 2).reshape(HT, WD, FR, CH)

    sg_other = send(saved_grad, to_half)
    cot_near = (cot, cot_other, cot_pair, cot_both)
    cot_swapped = send(jnp.stack(cot_near), to_core)
    sg_other, cot_swapped = together(sg_other, cot_swapped)

    arrays = (saved_grad, sg_other, spatial_kernel, sk_other, sk_other)
    up, down = blocks_of(True, (1, 3), *arrays)
    sg_late = after(saved_grad, up)
    up, down = send(up, to_z(1)), send(down, to_z(3))
    sg_pair, sg_both = send(sg_late, to_pair), send(sg_late, to_both)
    far, mine = blocks_of(True, (2, 0), *arrays, sg_late, *hidden_left)
    up, down, far, sg_pair, sg_both = together(up, down, far, sg_pair, sg_both)

    far = send(far, to_z(2))
    sg_near = (saved_grad, sg_other, sg_pair, sg_both)
    sg_swapped = send(jnp.stack(sg_near), to_core)

    slots = jnp.array([[0, 2, 1, 3], [2, 0, 3, 1]], jnp.int32)[half]
    temporal_parts = wgrad(False, 0, 3, slots, saved_left, cot_near + (cot_swapped,), up)
    temporal_total = lax.psum_scatter(
        temporal_parts, "dp", scatter_dimension=0, axis_index_groups=y_groups
    )
    far, sg_swapped = together(far, sg_swapped)
    order = (slots - y) % 4
    parts = wgrad(True, 0, 9, order, hidden_left, sg_near + (sg_swapped,), temporal_parts)
    hidden_grad = total_of(mine, (up, far, down))

    normed_grad = hidden_grad * gate * (1.0 + normed * (1.0 - gate))
    gain_sum = jnp.sum(normed_grad * normed_hat, axis=0)
    bias_sum = jnp.sum(normed_grad, axis=0)
    first = per_group(bias_sum * norm_gain) / count
    second = per_group(gain_sum * norm_gain) / count
    branch = inverse * (normed_grad * norm_gain - first - normed_hat * second)
    branch = branch.reshape(HT * WD, FR, CH).transpose(1, 0, 2)
    input_grad = (cot.astype(F32) + branch).astype(BF).reshape(block_input.shape)

    def to_owners(total):
        total = total.astype(BF)
        mine, other = total[:, :, :CH], total[:, :, CH:]
        same = half == core
        first, second = jnp.where(same, mine, other), jnp.where(same, other, mine)
        first, second = together(first, second)
        return send(first, to_owner(0)), send(second, to_owner(1))

    def owned(first, second):
        low, high = jnp.where(half == 0, first, second), jnp.where(half == 0, second, first)
        return jnp.concatenate([low, high], axis=1).astype(F32)

    sums = after(jnp.stack([gain_sum, bias_sum]), parts)
    sums = lax.all_gather(sums, "dp", axis=0)
    others = [send(parts[k], to_y(k)) for k in (1, 2, 3)]
    *others, sums = together(*others, sums)
    total = parts[0].astype(F32)
    for other in others:
        total = total + other.astype(F32)
    owned_parts = together(*to_owners(total), *to_owners(after(temporal_total, sums)))
    spatial_owned, temporal_owned = owned_parts[:2], owned_parts[2:]
    sums = jnp.sum(sums, axis=0)
    temporal_grad = owned(*temporal_owned)
    spatial_grad = owned(*spatial_owned).reshape(3, 3, CH // 2, CH)
    return (input_grad, spatial_grad, temporal_grad, sums[0], sums[1])


def solution(mesh):
    placed = (
        P("dp", None, None, None, "mp"),
        P("dp", None, None, None, "mp"),
        P("dp", None, None, None, "mp"),
        P(None, None, None, "mp"),
        P(None, None, "mp"),
        P("mp"),
        P("mp"),
    )
    return jax.shard_map(
        local,
        mesh=mesh,
        in_specs=placed,
        out_specs=(
            P("dp", None, None, None, "mp"),
            P(None, None, "dp", "mp"),
            P(None, "dp", "mp"),
            P("mp"),
            P("mp"),
        ),
        check_vma=False,
    )
```

```python
import itertools

import jax
import jax.numpy as jnp
from jax import lax
from jax.experimental import pallas as pl
from jax.experimental.pallas import tpu as pltpu
from jax.sharding import PartitionSpec as P

C = 2048
G = 32
FR = 16
HT = 8
WD = 8
EPSILON = 1e-05

ROWS = FR * HT * WD
CH = 256
SUB = 64
BF = jnp.bfloat16
F32 = jnp.float32
VMEM = 60 * 1024 * 1024


def linear(x, y, z, c):
    return (4 * y + 2 * (x % 2) + c) * 8 + 4 * (x // 2) + z


def send(value, to):
    pairs = []
    for x, y, z, c in itertools.product(range(4), range(4), range(4), range(2)):
        tx, ty, tz, tc = to(x, y, z, c)
        pairs.append((linear(x, y, z, c), linear(tx % 4, ty % 4, tz % 4, tc)))
    return lax.ppermute(value, ("dp", "mp"), pairs)


def to_z(step):
    return lambda x, y, z, c: (x, y, z + step, c)


def to_y(step):
    return lambda x, y, z, c: (x, y + step, z, c)


def to_core(x, y, z, c):
    return (x, y, z, 1 - c)


def to_half(x, y, z, c):
    return (x ^ 2, y, z, c)


def to_pair(x, y, z, c):
    return (x ^ 1, y, z, c)


def to_both(x, y, z, c):
    return (x ^ 3, y, z, c)


def to_pair_core(x, y, z, c):
    return (x ^ 1, y, z, 1 - c)


BLOCK_OF = ((0, 2, 1, 3), (1, 3, 0, 2))


def to_owner(flip):
    def to(x, y, z, c):
        half, pair = x // 2, x % 2
        block = BLOCK_OF[half][y]
        return (2 * (flip ^ c) + block % 2, 2 * half + block // 2, z, pair)

    return to


def contract_cols(left, right):
    return lax.dot_general(left, right, (((1,), (1,)), ((), ())), preferred_element_type=F32)


def contract_inner(left, right):
    return lax.dot_general(left, right, (((1,), (0,)), ((), ())), preferred_element_type=F32)


def cost(microseconds):
    return pl.CostEstimate(flops=int(microseconds * 1.15e9), bytes_accessed=0, transcendentals=0)


def params():
    return pltpu.CompilerParams(vmem_limit_bytes=VMEM)


def fill(padded, mine, other, spatial):
    if spatial:
        inner = (pl.ds(1, HT), pl.ds(1, WD), slice(None))
    else:
        inner = (pl.ds(1, FR), slice(None))
    padded[...] = jnp.zeros(padded.shape, BF)
    padded[inner + (pl.ds(0, CH),)] = mine
    padded[inner + (pl.ds(CH, CH),)] = other


def tap_rows(spatial, tap):
    if spatial:
        return (pl.ds(2 - tap // 3, HT), pl.ds(2 - tap % 3, WD))
    return (pl.ds(2 - tap, FR),)


def dgrad_body(spatial, blocks, index, mine, other, w_mine, *refs):
    w_other, outs, padded = refs[:2], refs[-1 - blocks : -1], refs[-1]
    step = pl.program_id(0)
    core = index[0]

    @pl.when(step == 0)
    def _():
        fill(padded, mine[...], other[...], spatial)

    total = jnp.zeros((ROWS, CH), F32)
    for tap in range(9 if spatial else 3):
        rows = padded[tap_rows(spatial, tap)].reshape(ROWS, 2 * CH)
        near, far = [w[0, tap] for w in w_other]
        low = jnp.where(core == 0, near, far)
        high = jnp.where(core == 0, far, near)
        weights = jnp.concatenate([w_mine[tap], jnp.concatenate([low, high], axis=0)], axis=1)
        total = total + contract_cols(rows, weights)
    for place, out in enumerate(outs):

        @pl.when(step == place)
        def _():
            out[...] = total.astype(out.dtype)


def whole(shape):
    return pl.BlockSpec(shape, lambda i, ix: (0,) * len(shape))


def pad_shape(spatial):
    return (HT + 2, WD + 2, FR, 2 * CH) if spatial else (FR + 2, HT * WD, 2 * CH)


def dgrad(spatial, blocks, kinds, index, mine, other, w_mine, w_near, w_far, *waits):
    taps = 9 if spatial else 3
    near = pl.BlockSpec((1, taps, CH // 2, CH), lambda i, ix: (ix[1 + blocks + i], 0, 0, 0))
    far = pl.BlockSpec((1, taps, CH // 2, CH), lambda i, ix: (ix[1 + 2 * blocks + i], 0, 0, 0))
    return pl.pallas_call(
        lambda *refs: dgrad_body(spatial, blocks, *refs),
        grid_spec=pltpu.PrefetchScalarGridSpec(
            num_scalar_prefetch=1,
            grid=(blocks,),
            in_specs=[
                whole(mine.shape),
                whole(other.shape),
                pl.BlockSpec((taps, CH, CH), lambda i, ix: (0, ix[1 + i], 0)),
                near,
                far,
            ]
            + [pl.BlockSpec(memory_space=pl.ANY)] * len(waits),
            out_specs=[whole((ROWS, CH))] * blocks,
            scratch_shapes=[pltpu.VMEM(pad_shape(spatial), BF)],
        ),
        out_shape=[jax.ShapeDtypeStruct((ROWS, CH), kind) for kind in kinds],
        compiler_params=params(),
        cost_estimate=cost(2.0 + 3.2 * blocks if spatial else 7.0),
    )(index, mine, other, w_mine, w_near, w_far, *waits)


def wgrad_body(first, spatial, lefts, index, *refs):
    left, (mine, other, pair, both, swapped) = refs[:lefts], refs[lefts : lefts + 5]
    outs, padded = refs[-5:-1] if spatial else refs[-2:-1], refs[-1]
    step = pl.program_id(0)

    @pl.when(step == 0)
    def _():
        fill(padded.at[0], mine[...], other[...], spatial)
        fill(padded.at[1], swapped[0], swapped[1], spatial)
        fill(padded.at[2], pair[...], both[...], spatial)
        fill(padded.at[3], swapped[2], swapped[3], spatial)

    right = padded[(slice(None),) + tap_rows(spatial, step + first)]
    blocks = jnp.concatenate([ref[...].reshape(-1, 4 * ROWS) for ref in left], axis=0)
    result = contract_inner(blocks, right.reshape(4 * ROWS, 2 * CH))
    result = result.astype(BF)
    if not spatial:
        for block in range(4):
            outs[0][index[block], 0] = result[block * SUB : (block + 1) * SUB]
        return
    for block in range(4):
        for place in range(4):

            @pl.when(index[block] == place)
            def _():
                outs[place][0] = result[block * SUB : (block + 1) * SUB]


def wgrad(spatial, first, taps, index, left, fields, *waits):
    if spatial:
        out_specs = [pl.BlockSpec((1, SUB, 2 * CH), lambda i, ix: (i, 0, 0))] * 4
        out_shape = [jax.ShapeDtypeStruct((taps, SUB, 2 * CH), BF)] * 4
    else:
        out_specs = pl.BlockSpec((4, 1, SUB, 2 * CH), lambda i, ix: (0, i, 0, 0))
        out_shape = jax.ShapeDtypeStruct((4, taps, SUB, 2 * CH), BF)
    return pl.pallas_call(
        lambda *refs: wgrad_body(first, spatial, len(left), *refs),
        grid_spec=pltpu.PrefetchScalarGridSpec(
            num_scalar_prefetch=1,
            grid=(taps,),
            in_specs=[whole(f.shape) for f in left + fields]
            + [pl.BlockSpec(memory_space=pl.ANY)] * len(waits),
            out_specs=out_specs,
            scratch_shapes=[pltpu.VMEM((4,) + pad_shape(spatial), BF)],
        ),
        out_shape=out_shape,
        compiler_params=params(),
        cost_estimate=cost(4.7 + 1.25 * taps),
    )(index, *left, *fields, *waits)


def after(value, *others):
    return pl.pallas_call(
        lambda *refs: None,
        in_specs=[pl.BlockSpec(memory_space=pl.ANY)] * (1 + len(others)),
        out_specs=pl.BlockSpec(memory_space=pl.ANY),
        out_shape=jax.ShapeDtypeStruct(value.shape, value.dtype),
        input_output_aliases={0: 0},
        cost_estimate=pl.CostEstimate(flops=0, bytes_accessed=0, transcendentals=0),
    )(value, *others)


def together(*values):
    return pl.pallas_call(
        lambda *refs: None,
        in_specs=[pl.BlockSpec(memory_space=pl.ANY)] * len(values),
        out_specs=[pl.BlockSpec(memory_space=pl.ANY)] * len(values),
        out_shape=[jax.ShapeDtypeStruct(value.shape, value.dtype) for value in values],
        input_output_aliases={i: i for i in range(len(values))},
        cost_estimate=pl.CostEstimate(flops=0, bytes_accessed=0, transcendentals=0),
    )(*values)


def per_group(values):
    return jnp.repeat(jnp.sum(values.reshape(-1, C // G), axis=1), C // G)


def local(
    block_input, spatial_out, cotangent, spatial_kernel, temporal_kernel, norm_gain, norm_bias
):
    dp, mp = lax.axis_index("dp"), lax.axis_index("mp")
    y, pair, core = dp // 4, (dp // 2) % 2, dp % 2
    half, z = mp // 4, mp % 4
    quarter = 2 * pair + core
    y_core_groups = [[4 * a + 2 * p + b for a in range(4) for b in range(2)] for p in range(2)]
    y_groups = [[4 * a + b for a in range(4)] for b in range(4)]
    z_groups = [[0, 1, 2, 3], [4, 5, 6, 7]]

    cot = cotangent.reshape(FR, HT * WD, CH)
    spatial_kernel = spatial_kernel.reshape(9, C, CH)

    def exchange(turned):
        pick = lambda k: lax.dynamic_index_in_dim(turned, quarter ^ k, 0, keepdims=False)
        sent = send(pick(1), to_core), send(pick(2), to_pair), send(pick(3), to_pair_core)
        return pick(0), sent

    def kernel_part(kernel):
        start = (1 - half) * 1024 + y * 256 + core * 128
        return lax.dynamic_slice_in_dim(kernel, start, 128, axis=1)

    tk_part = send(kernel_part(temporal_kernel), to_half)
    tk_parts = [send(tk_part, to_y(k)) for k in (1, 2, 3)]
    cot_other = send(after(cot, tk_part), to_half)
    turned = spatial_out.reshape(ROWS, CH).T.reshape(4, SUB, ROWS)
    own, parts = exchange(after(turned, tk_part))
    cot_other, tk_one, tk_two, tk_three, *parts = together(cot_other, *tk_parts, *parts)
    tk_near = jnp.stack([tk_part, tk_one, tk_two, tk_three])
    saved_part = jnp.concatenate([own, *parts], axis=1)
    saved_left = (lax.all_gather(saved_part, "mp", axis=0, axis_index_groups=z_groups),)

    flat_in = block_input.reshape(FR, HT * WD, CH).transpose(1, 0, 2).reshape(ROWS, CH).astype(F32)
    count = ROWS * (C // G)
    center = per_group(jnp.sum(flat_in, axis=0)) / count
    spread = per_group(jnp.sum(jnp.square(flat_in - center), axis=0)) / count
    inverse = lax.rsqrt(spread + EPSILON)
    normed_hat = (flat_in - center) * inverse
    normed = normed_hat * norm_gain + norm_bias
    gate = jax.nn.sigmoid(normed)
    hidden = (normed * gate).astype(BF)

    def blocks_of(spatial, steps, *arrays):
        blocks = [(z + k) % 4 for k in steps]
        if spatial:
            near, far = [2 * b for b in blocks], [2 * b + 1 for b in blocks]
        else:
            near = far = [(y - b) % 4 for b in blocks]
        index = [0 if spatial else core] + [half * 4 + b for b in blocks] + near + far
        index = jnp.stack([jnp.int32(i) for i in index])
        kinds = [BF if k else F32 for k in steps]
        return dgrad(spatial, len(steps), kinds, index, *arrays)

    def total_of(mine, sent):
        one, two, three = [v.astype(F32) for v in sent]
        return mine + (one + three) + two

    tk_far = send(tk_near, to_core)
    arrays = (cot, cot_other, temporal_kernel, tk_near, tk_far)
    sk_part = send(after(kernel_part(spatial_kernel), tk_far), to_half)
    up, down, far, mine = blocks_of(False, (1, 3, 2, 0), *arrays)
    sk_part, up, down, far = together(sk_part, up, down, far)
    sk_other = lax.all_gather(sk_part, "dp", axis=0, axis_index_groups=y_core_groups)

    up, down = send(up, to_z(1)), send(down, to_z(3))
    cot_late = after(cot, mine)
    cot_pair, cot_both = send(cot_late, to_pair), send(cot_late, to_both)
    up, down, far, cot_pair, cot_both = together(up, down, far, cot_pair, cot_both)

    far = send(far, to_z(2))
    cot_near = (cot, cot_other, cot_pair, cot_both)
    cot_swapped = send(jnp.stack(cot_near), to_core)
    own, parts = exchange(after(hidden.T.reshape(4, SUB, ROWS), up))
    far, cot_swapped, *parts = together(far, cot_swapped, *parts)
    hidden_part = jnp.concatenate([own, *parts], axis=1)
    hidden_left = (lax.all_gather(hidden_part, "mp", axis=0, axis_index_groups=z_groups),)
    saved_grad = total_of(mine, (up, far, down)).astype(BF)
    saved_grad = saved_grad.reshape(FR, HT * WD, CH).transpose(1, 0, 2).reshape(HT, WD, FR, CH)

    sg_other = send(saved_grad, to_half)
    slots = jnp.array([[0, 2, 1, 3], [2, 0, 3, 1]], jnp.int32)[half]
    fields = cot_near + (cot_swapped,)
    temporal_parts = wgrad(False, 0, 3, slots, saved_left, fields, saved_grad)
    sg_other, temporal_parts = together(sg_other, temporal_parts)
    temporal_total = lax.psum_scatter(
        temporal_parts, "dp", scatter_dimension=0, axis_index_groups=y_groups
    )

    arrays = (saved_grad, sg_other, spatial_kernel, sk_other, sk_other)
    up, down = blocks_of(True, (1, 3), *arrays)
    sg_late = after(saved_grad, up)
    up, down = send(up, to_z(1)), send(down, to_z(3))
    sg_pair, sg_both = send(sg_late, to_pair), send(sg_late, to_both)
    far, mine = blocks_of(True, (2, 0), *arrays, sg_late)
    up, down, far, sg_pair, sg_both = together(up, down, far, sg_pair, sg_both)

    sg_near = (saved_grad, sg_other, sg_pair, sg_both)
    sg_fields = sg_near + (send(jnp.stack(sg_near), to_core),)
    far = send(far, to_z(2))
    parts = wgrad(True, 0, 9, (slots - y) % 4, hidden_left, sg_fields)
    far, *parts = together(far, *parts)
    hidden_grad = total_of(mine, (up, far, down))

    normed_grad = hidden_grad * gate * (1.0 + normed * (1.0 - gate))
    gain_sum = jnp.sum(normed_grad * normed_hat, axis=0)
    bias_sum = jnp.sum(normed_grad, axis=0)
    first = per_group(bias_sum * norm_gain) / count
    second = per_group(gain_sum * norm_gain) / count
    branch = inverse * (normed_grad * norm_gain - first - normed_hat * second)
    branch = branch.reshape(HT * WD, FR, CH).transpose(1, 0, 2)
    input_grad = (cot.astype(F32) + branch).astype(BF).reshape(block_input.shape)

    def to_owners(total):
        total = total.astype(BF)
        mine, other = total[:, :, :CH], total[:, :, CH:]
        same = half == core
        first, second = jnp.where(same, mine, other), jnp.where(same, other, mine)
        first, second = together(first, second)
        return send(first, to_owner(0)), send(second, to_owner(1))

    def owned(first, second):
        low, high = jnp.where(half == 0, first, second), jnp.where(half == 0, second, first)
        return jnp.concatenate([low, high], axis=1).astype(F32)

    sums = lax.all_gather(jnp.stack([gain_sum, bias_sum]), "dp", axis=0)
    temporal_owned = to_owners(after(temporal_total, parts[0]))
    others = [send(parts[k], to_y(k)) for k in (1, 2, 3)]
    *others, sums, tk_first, tk_second = together(*others, sums, *temporal_owned)
    total = parts[0].astype(F32)
    for other in others:
        total = total + other.astype(F32)
    first, second = to_owners(total)
    sums = jnp.sum(sums, axis=0)
    temporal_grad = owned(tk_first, tk_second)
    spatial_grad = owned(first, second).reshape(3, 3, CH // 2, CH)
    return (input_grad, spatial_grad, temporal_grad, sums[0], sums[1])


def solution(mesh):
    placed = (
        P("dp", None, None, None, "mp"),
        P("dp", None, None, None, "mp"),
        P("dp", None, None, None, "mp"),
        P(None, None, None, "mp"),
        P(None, None, "mp"),
        P("mp"),
        P("mp"),
    )
    return jax.shard_map(
        local,
        mesh=mesh,
        in_specs=placed,
        out_specs=(
            P("dp", None, None, None, "mp"),
            P(None, None, "dp", "mp"),
            P(None, "dp", "mp"),
            P("mp"),
            P("mp"),
        ),
        check_vma=False,
    )
```

```python
import itertools

import jax
import jax.numpy as jnp
from jax import lax
from jax.experimental import pallas as pl
from jax.experimental.pallas import tpu as pltpu
from jax.sharding import PartitionSpec as P

C = 2048
G = 32
FR = 16
HT = 8
WD = 8
EPSILON = 1e-05

ROWS = FR * HT * WD
CH = 256
SUB = 64
BF = jnp.bfloat16
F32 = jnp.float32
VMEM = 60 * 1024 * 1024


def linear(x, y, z, c):
    return (4 * y + 2 * (x % 2) + c) * 8 + 4 * (x // 2) + z


def send(value, to):
    pairs = []
    for x, y, z, c in itertools.product(range(4), range(4), range(4), range(2)):
        tx, ty, tz, tc = to(x, y, z, c)
        pairs.append((linear(x, y, z, c), linear(tx % 4, ty % 4, tz % 4, tc)))
    return lax.ppermute(value, ("dp", "mp"), pairs)


def to_z(step):
    return lambda x, y, z, c: (x, y, z + step, c)


def to_y(step):
    return lambda x, y, z, c: (x, y + step, z, c)


def to_core(x, y, z, c):
    return (x, y, z, 1 - c)


def to_half(x, y, z, c):
    return (x ^ 2, y, z, c)


def to_pair(x, y, z, c):
    return (x ^ 1, y, z, c)


def to_both(x, y, z, c):
    return (x ^ 3, y, z, c)


def to_pair_core(x, y, z, c):
    return (x ^ 1, y, z, 1 - c)


BLOCK_OF = ((0, 2, 1, 3), (1, 3, 0, 2))


def to_owner(flip):
    def to(x, y, z, c):
        half, pair = x // 2, x % 2
        block = BLOCK_OF[half][y]
        return (2 * (flip ^ c) + block % 2, 2 * half + block // 2, z, pair)

    return to


def contract_cols(left, right):
    return lax.dot_general(left, right, (((1,), (1,)), ((), ())), preferred_element_type=F32)


def contract_inner(left, right):
    return lax.dot_general(left, right, (((1,), (0,)), ((), ())), preferred_element_type=F32)


def cost(microseconds):
    return pl.CostEstimate(flops=int(microseconds * 1.15e9), bytes_accessed=0, transcendentals=0)


def params():
    return pltpu.CompilerParams(vmem_limit_bytes=VMEM)


def fill(padded, mine, other, spatial):
    if spatial:
        inner = (pl.ds(1, HT), pl.ds(1, WD), slice(None))
        for edge in (0, HT + 1):
            padded[edge] = jnp.zeros((WD + 2, FR, 2 * CH), BF)
        for edge in (0, WD + 1):
            padded[pl.ds(1, HT), pl.ds(edge, 1)] = jnp.zeros((HT, 1, FR, 2 * CH), BF)
    else:
        inner = (pl.ds(1, FR), slice(None))
        for edge in (0, FR + 1):
            padded[edge] = jnp.zeros((HT * WD, 2 * CH), BF)
    padded[inner + (pl.ds(0, CH),)] = mine
    padded[inner + (pl.ds(CH, CH),)] = other


def tap_rows(spatial, tap):
    if spatial:
        return (pl.ds(2 - tap // 3, HT), pl.ds(2 - tap % 3, WD))
    return (pl.ds(2 - tap, FR),)


def dgrad_body(spatial, blocks, index, mine, other, w_mine, *refs):
    w_other, outs, padded = refs[:2], refs[-1 - blocks : -1], refs[-1]
    step = pl.program_id(0)
    core = index[0]

    @pl.when(step == 0)
    def _():
        fill(padded, mine[...], other[...], spatial)

    total = jnp.zeros((ROWS, CH), F32)
    for tap in range(9 if spatial else 3):
        rows = padded[tap_rows(spatial, tap)].reshape(ROWS, 2 * CH)
        near, far = [w[0, tap] for w in w_other]
        low = jnp.where(core == 0, near, far)
        high = jnp.where(core == 0, far, near)
        weights = jnp.concatenate([w_mine[tap], jnp.concatenate([low, high], axis=0)], axis=1)
        total = total + contract_cols(rows, weights)
    for place, out in enumerate(outs):

        @pl.when(step == place)
        def _():
            out[...] = total.astype(out.dtype)


def whole(shape):
    return pl.BlockSpec(shape, lambda i, ix: (0,) * len(shape))


def pad_shape(spatial):
    return (HT + 2, WD + 2, FR, 2 * CH) if spatial else (FR + 2, HT * WD, 2 * CH)


def dgrad(spatial, blocks, kinds, index, mine, other, w_mine, w_near, w_far, *waits):
    taps = 9 if spatial else 3
    near = pl.BlockSpec((1, taps, CH // 2, CH), lambda i, ix: (ix[1 + blocks + i], 0, 0, 0))
    far = pl.BlockSpec((1, taps, CH // 2, CH), lambda i, ix: (ix[1 + 2 * blocks + i], 0, 0, 0))
    return pl.pallas_call(
        lambda *refs: dgrad_body(spatial, blocks, *refs),
        grid_spec=pltpu.PrefetchScalarGridSpec(
            num_scalar_prefetch=1,
            grid=(blocks,),
            in_specs=[
                whole(mine.shape),
                whole(other.shape),
                pl.BlockSpec((taps, CH, CH), lambda i, ix: (0, ix[1 + i], 0)),
                near,
                far,
            ]
            + [pl.BlockSpec(memory_space=pl.ANY)] * len(waits),
            out_specs=[whole((ROWS, CH))] * blocks,
            scratch_shapes=[pltpu.VMEM(pad_shape(spatial), BF)],
        ),
        out_shape=[jax.ShapeDtypeStruct((ROWS, CH), kind) for kind in kinds],
        compiler_params=params(),
        cost_estimate=cost(2.0 + 3.2 * blocks if spatial else 7.0),
    )(index, mine, other, w_mine, w_near, w_far, *waits)


def wgrad_body(first, spatial, lefts, fields, index, *refs):
    left, (mine, other, pair, both, *swapped) = refs[:lefts], refs[lefts : lefts + fields]
    if len(swapped) == 1:
        swapped = [swapped[0].at[i] for i in range(4)]
    outs, padded = refs[-5:-1] if spatial else refs[-2:-1], refs[-1]
    step = pl.program_id(0)

    @pl.when(step == 0)
    def _():
        fill(padded.at[0], mine[...], other[...], spatial)
        fill(padded.at[1], swapped[0][...], swapped[1][...], spatial)
        fill(padded.at[2], pair[...], both[...], spatial)
        fill(padded.at[3], swapped[2][...], swapped[3][...], spatial)

    right = padded[(slice(None),) + tap_rows(spatial, step + first)]
    blocks = jnp.concatenate([ref[...].reshape(-1, 4 * ROWS) for ref in left], axis=0)
    result = contract_inner(blocks, right.reshape(4 * ROWS, 2 * CH))
    result = result.astype(BF)
    if not spatial:
        for block in range(4):
            outs[0][index[block], 0] = result[block * SUB : (block + 1) * SUB]
        return
    for block in range(4):
        for place in range(4):

            @pl.when(index[block] == place)
            def _():
                outs[place][0] = result[block * SUB : (block + 1) * SUB]


def wgrad(spatial, first, taps, index, left, fields, *waits):
    if spatial:
        out_specs = [pl.BlockSpec((1, SUB, 2 * CH), lambda i, ix: (i, 0, 0))] * 4
        out_shape = [jax.ShapeDtypeStruct((taps, SUB, 2 * CH), BF)] * 4
    else:
        out_specs = pl.BlockSpec((4, 1, SUB, 2 * CH), lambda i, ix: (0, i, 0, 0))
        out_shape = jax.ShapeDtypeStruct((4, taps, SUB, 2 * CH), BF)
    return pl.pallas_call(
        lambda *refs: wgrad_body(first, spatial, len(left), len(fields), *refs),
        grid_spec=pltpu.PrefetchScalarGridSpec(
            num_scalar_prefetch=1,
            grid=(taps,),
            in_specs=[whole(f.shape) for f in left + fields]
            + [pl.BlockSpec(memory_space=pl.ANY)] * len(waits),
            out_specs=out_specs,
            scratch_shapes=[pltpu.VMEM((4,) + pad_shape(spatial), BF)],
        ),
        out_shape=out_shape,
        compiler_params=params(),
        cost_estimate=cost(4.7 + 1.25 * taps),
    )(index, *left, *fields, *waits)


def after(value, *others):
    return pl.pallas_call(
        lambda *refs: None,
        in_specs=[pl.BlockSpec(memory_space=pl.ANY)] * (1 + len(others)),
        out_specs=pl.BlockSpec(memory_space=pl.ANY),
        out_shape=jax.ShapeDtypeStruct(value.shape, value.dtype),
        input_output_aliases={0: 0},
        cost_estimate=pl.CostEstimate(flops=0, bytes_accessed=0, transcendentals=0),
    )(value, *others)


def together(*values):
    return pl.pallas_call(
        lambda *refs: None,
        in_specs=[pl.BlockSpec(memory_space=pl.ANY)] * len(values),
        out_specs=[pl.BlockSpec(memory_space=pl.ANY)] * len(values),
        out_shape=[jax.ShapeDtypeStruct(value.shape, value.dtype) for value in values],
        input_output_aliases={i: i for i in range(len(values))},
        cost_estimate=pl.CostEstimate(flops=0, bytes_accessed=0, transcendentals=0),
    )(*values)


def per_group(values):
    return jnp.repeat(jnp.sum(values.reshape(-1, C // G), axis=1), C // G)


def local(
    block_input, spatial_out, cotangent, spatial_kernel, temporal_kernel, norm_gain, norm_bias
):
    dp, mp = lax.axis_index("dp"), lax.axis_index("mp")
    y, pair, core = dp // 4, (dp // 2) % 2, dp % 2
    half, z = mp // 4, mp % 4
    quarter = 2 * pair + core
    y_core_groups = [[4 * a + 2 * p + b for a in range(4) for b in range(2)] for p in range(2)]
    y_groups = [[4 * a + b for a in range(4)] for b in range(4)]
    z_groups = [[0, 1, 2, 3], [4, 5, 6, 7]]

    cot = cotangent.reshape(FR, HT * WD, CH)
    spatial_kernel = spatial_kernel.reshape(9, C, CH)

    def exchange(turned):
        pick = lambda k: lax.dynamic_index_in_dim(turned, quarter ^ k, 0, keepdims=False)
        sent = send(pick(1), to_core), send(pick(2), to_pair), send(pick(3), to_pair_core)
        return pick(0), sent

    def kernel_part(kernel):
        start = (1 - half) * 1024 + y * 256 + core * 128
        return lax.dynamic_slice_in_dim(kernel, start, 128, axis=1)

    tk_part = send(kernel_part(temporal_kernel), to_half)
    tk_parts = [send(tk_part, to_y(k)) for k in (1, 2, 3)]
    cot_other = send(after(cot, tk_part), to_half)
    turned = spatial_out.reshape(ROWS, CH).T.reshape(4, SUB, ROWS)
    own, parts = exchange(after(turned, tk_part))
    cot_other, tk_one, tk_two, tk_three, *parts = together(cot_other, *tk_parts, *parts)
    tk_near = jnp.stack([tk_part, tk_one, tk_two, tk_three])
    saved_part = jnp.concatenate([own, *parts], axis=1)
    saved_left = (lax.all_gather(saved_part, "mp", axis=0, axis_index_groups=z_groups),)

    flat_in = block_input.reshape(FR, HT * WD, CH).transpose(1, 0, 2).reshape(ROWS, CH).astype(F32)
    count = ROWS * (C // G)
    center = per_group(jnp.sum(flat_in, axis=0)) / count
    spread = per_group(jnp.sum(jnp.square(flat_in - center), axis=0)) / count
    inverse = lax.rsqrt(spread + EPSILON)
    normed_hat = (flat_in - center) * inverse
    normed = normed_hat * norm_gain + norm_bias
    gate = jax.nn.sigmoid(normed)
    hidden = (normed * gate).astype(BF)

    def blocks_of(spatial, steps, *arrays):
        blocks = [(z + k) % 4 for k in steps]
        if spatial:
            near, far = [2 * b for b in blocks], [2 * b + 1 for b in blocks]
        else:
            near = far = [(y - b) % 4 for b in blocks]
        index = [0 if spatial else core] + [half * 4 + b for b in blocks] + near + far
        index = jnp.stack([jnp.int32(i) for i in index])
        kinds = [BF if k else F32 for k in steps]
        return dgrad(spatial, len(steps), kinds, index, *arrays)

    def total_of(mine, sent):
        one, two, three = [v.astype(F32) for v in sent]
        return mine + (one + three) + two

    tk_far = send(tk_near, to_core)
    arrays = (cot, cot_other, temporal_kernel, tk_near, tk_far)
    sk_part = send(after(kernel_part(spatial_kernel), tk_far), to_half)
    up, down, far, mine = blocks_of(False, (1, 3, 2, 0), *arrays)
    sk_part, up, down, far = together(sk_part, up, down, far)
    sk_other = lax.all_gather(sk_part, "dp", axis=0, axis_index_groups=y_core_groups)

    up, down = send(up, to_z(1)), send(down, to_z(3))
    cot_late = after(cot, mine)
    cot_pair, cot_both = send(cot_late, to_pair), send(cot_late, to_both)
    up, down, far, cot_pair, cot_both = together(up, down, far, cot_pair, cot_both)

    own, parts = exchange(after(hidden.T.reshape(4, SUB, ROWS), up))
    cot_near = (cot, cot_other, cot_pair, cot_both)
    cot_swapped = send(jnp.stack(cot_near), to_core)
    far = send(far, to_z(2))
    cot_swapped, *parts, far = together(cot_swapped, *parts, far)
    hidden_part = jnp.concatenate([own, *parts], axis=1)
    hidden_left = (lax.all_gather(hidden_part, "mp", axis=0, axis_index_groups=z_groups),)
    saved_grad = total_of(mine, (up, far, down)).astype(BF)
    saved_grad = saved_grad.reshape(FR, HT * WD, CH).transpose(1, 0, 2).reshape(HT, WD, FR, CH)

    sg_other = send(saved_grad, to_half)
    slots = jnp.array([[0, 2, 1, 3], [2, 0, 3, 1]], jnp.int32)[half]
    fields = cot_near + (cot_swapped,)
    temporal_parts = wgrad(False, 0, 3, slots, saved_left, fields, saved_grad)
    sg_other, temporal_parts = together(sg_other, temporal_parts)
    temporal_total = lax.psum_scatter(
        temporal_parts, "dp", scatter_dimension=0, axis_index_groups=y_groups
    )

    arrays = (saved_grad, sg_other, spatial_kernel, sk_other, sk_other)
    up, down = blocks_of(True, (1, 3), *arrays)
    sg_late = after(saved_grad, up)
    up, down = send(up, to_z(1)), send(down, to_z(3))
    sg_pair, sg_both = send(sg_late, to_pair), send(sg_late, to_both)
    far, mine = blocks_of(True, (2, 0), *arrays, sg_late)
    up, down, far, sg_pair, sg_both = together(up, down, far, sg_pair, sg_both)

    sg_near = (saved_grad, sg_other, sg_pair, sg_both)
    far = send(far, to_z(2))
    sg_fields = sg_near + tuple(send(value, to_core) for value in sg_near)
    parts = wgrad(True, 0, 9, (slots - y) % 4, hidden_left, sg_fields)
    far, *parts = together(far, *parts)
    hidden_grad = total_of(mine, (up, far, down))

    normed_grad = hidden_grad * gate * (1.0 + normed * (1.0 - gate))
    gain_sum = jnp.sum(normed_grad * normed_hat, axis=0)
    bias_sum = jnp.sum(normed_grad, axis=0)
    first = per_group(bias_sum * norm_gain) / count
    second = per_group(gain_sum * norm_gain) / count
    branch = inverse * (normed_grad * norm_gain - first - normed_hat * second)
    branch = branch.reshape(HT * WD, FR, CH).transpose(1, 0, 2)
    input_grad = (cot.astype(F32) + branch).astype(BF).reshape(block_input.shape)

    def to_owners(total):
        total = total.astype(BF)
        mine, other = total[:, :, :CH], total[:, :, CH:]
        same = half == core
        first, second = jnp.where(same, mine, other), jnp.where(same, other, mine)
        first, second = together(first, second)
        return send(first, to_owner(0)), send(second, to_owner(1))

    def owned(first, second):
        low, high = jnp.where(half == 0, first, second), jnp.where(half == 0, second, first)
        return jnp.concatenate([low, high], axis=1).astype(F32)

    sums = lax.all_gather(jnp.stack([gain_sum, bias_sum]), "dp", axis=0)
    others = [send(parts[k], to_y(k)) for k in (1, 2, 3)]
    *others, sums = together(*others, sums)
    total = parts[0].astype(F32)
    for other in others:
        total = total + other.astype(F32)
    temporal_total = after(temporal_total, parts[0])
    grads = owned(*to_owners(jnp.concatenate([total.astype(BF), temporal_total])))
    spatial_grad, temporal_grad = grads[:9].reshape(3, 3, CH // 2, CH), grads[9:]
    sums = jnp.sum(sums, axis=0)
    return (input_grad, spatial_grad, temporal_grad, sums[0], sums[1])


def solution(mesh):
    placed = (
        P("dp", None, None, None, "mp"),
        P("dp", None, None, None, "mp"),
        P("dp", None, None, None, "mp"),
        P(None, None, None, "mp"),
        P(None, None, "mp"),
        P("mp"),
        P("mp"),
    )
    return jax.shard_map(
        local,
        mesh=mesh,
        in_specs=placed,
        out_specs=(
            P("dp", None, None, None, "mp"),
            P(None, None, "dp", "mp"),
            P(None, "dp", "mp"),
            P("mp"),
            P("mp"),
        ),
        check_vma=False,
    )
```

```python
import itertools

import jax
import jax.numpy as jnp
from jax import lax
from jax.experimental import pallas as pl
from jax.experimental.pallas import tpu as pltpu
from jax.sharding import PartitionSpec as P

C = 2048
G = 32
FR = 16
HT = 8
WD = 8
EPSILON = 1e-05

ROWS = FR * HT * WD
CH = 256
SUB = 64
BF = jnp.bfloat16
F32 = jnp.float32
VMEM = 60 * 1024 * 1024


def linear(x, y, z, c):
    return (4 * y + 2 * (x % 2) + c) * 8 + 4 * (x // 2) + z


def send(value, to):
    pairs = []
    for x, y, z, c in itertools.product(range(4), range(4), range(4), range(2)):
        tx, ty, tz, tc = to(x, y, z, c)
        pairs.append((linear(x, y, z, c), linear(tx % 4, ty % 4, tz % 4, tc)))
    return lax.ppermute(value, ("dp", "mp"), pairs)


def to_z(step):
    return lambda x, y, z, c: (x, y, z + step, c)


def to_y(step):
    return lambda x, y, z, c: (x, y + step, z, c)


def to_core(x, y, z, c):
    return (x, y, z, 1 - c)


def to_half(x, y, z, c):
    return (x ^ 2, y, z, c)


def to_pair(x, y, z, c):
    return (x ^ 1, y, z, c)


def to_both(x, y, z, c):
    return (x ^ 3, y, z, c)


def to_pair_core(x, y, z, c):
    return (x ^ 1, y, z, 1 - c)


BLOCK_OF = ((0, 2, 1, 3), (1, 3, 0, 2))


def to_owner(flip):
    def to(x, y, z, c):
        half, pair = x // 2, x % 2
        block = BLOCK_OF[half][y]
        return (2 * (flip ^ c) + block % 2, 2 * half + block // 2, z, pair)

    return to


def contract_cols(left, right):
    return lax.dot_general(left, right, (((1,), (1,)), ((), ())), preferred_element_type=F32)


def contract_inner(left, right):
    return lax.dot_general(left, right, (((1,), (0,)), ((), ())), preferred_element_type=F32)


def cost(microseconds):
    return pl.CostEstimate(flops=int(microseconds * 1.15e9), bytes_accessed=0, transcendentals=0)


def params():
    return pltpu.CompilerParams(vmem_limit_bytes=VMEM)


def fill(padded, mine, other, spatial):
    if spatial:
        inner = (pl.ds(1, HT), pl.ds(1, WD), slice(None))
        for edge in (0, HT + 1):
            padded[edge] = jnp.zeros((WD + 2, FR, 2 * CH), BF)
        for edge in (0, WD + 1):
            padded[pl.ds(1, HT), pl.ds(edge, 1)] = jnp.zeros((HT, 1, FR, 2 * CH), BF)
    else:
        inner = (pl.ds(1, FR), slice(None))
        for edge in (0, FR + 1):
            padded[edge] = jnp.zeros((HT * WD, 2 * CH), BF)
    padded[inner + (pl.ds(0, CH),)] = mine
    padded[inner + (pl.ds(CH, CH),)] = other


def tap_rows(spatial, tap):
    if spatial:
        return (pl.ds(2 - tap // 3, HT), pl.ds(2 - tap % 3, WD))
    return (pl.ds(2 - tap, FR),)


def dgrad_body(spatial, blocks, index, mine, other, w_mine, *refs):
    w_other, outs, padded = refs[:2], refs[-1 - blocks : -1], refs[-1]
    step = pl.program_id(0)
    core = index[0]

    @pl.when(step == 0)
    def _():
        fill(padded, mine[...], other[...], spatial)

    total = jnp.zeros((ROWS, CH), F32)
    for tap in range(9 if spatial else 3):
        rows = padded[tap_rows(spatial, tap)].reshape(ROWS, 2 * CH)
        near, far = [w[0, tap] for w in w_other]
        low = jnp.where(core == 0, near, far)
        high = jnp.where(core == 0, far, near)
        weights = jnp.concatenate([w_mine[tap], jnp.concatenate([low, high], axis=0)], axis=1)
        total = total + contract_cols(rows, weights)
    for place, out in enumerate(outs):

        @pl.when(step == place)
        def _():
            out[...] = total.astype(out.dtype)


def whole(shape):
    return pl.BlockSpec(shape, lambda i, ix: (0,) * len(shape))


def pad_shape(spatial):
    return (HT + 2, WD + 2, FR, 2 * CH) if spatial else (FR + 2, HT * WD, 2 * CH)


def dgrad(spatial, blocks, kinds, index, mine, other, w_mine, w_near, w_far, *waits):
    taps = 9 if spatial else 3
    near = pl.BlockSpec((1, taps, CH // 2, CH), lambda i, ix: (ix[1 + blocks + i], 0, 0, 0))
    far = pl.BlockSpec((1, taps, CH // 2, CH), lambda i, ix: (ix[1 + 2 * blocks + i], 0, 0, 0))
    return pl.pallas_call(
        lambda *refs: dgrad_body(spatial, blocks, *refs),
        grid_spec=pltpu.PrefetchScalarGridSpec(
            num_scalar_prefetch=1,
            grid=(blocks,),
            in_specs=[
                whole(mine.shape),
                whole(other.shape),
                pl.BlockSpec((taps, CH, CH), lambda i, ix: (0, ix[1 + i], 0)),
                near,
                far,
            ]
            + [pl.BlockSpec(memory_space=pl.ANY)] * len(waits),
            out_specs=[whole((ROWS, CH))] * blocks,
            scratch_shapes=[pltpu.VMEM(pad_shape(spatial), BF)],
        ),
        out_shape=[jax.ShapeDtypeStruct((ROWS, CH), kind) for kind in kinds],
        compiler_params=params(),
        cost_estimate=cost(2.0 + 3.2 * blocks if spatial else 7.0),
    )(index, mine, other, w_mine, w_near, w_far, *waits)


def wgrad_body(first, spatial, lefts, fields, index, *refs):
    left, (mine, other, pair, both, *swapped) = refs[:lefts], refs[lefts : lefts + fields]
    if len(swapped) == 1:
        swapped = [swapped[0].at[i] for i in range(4)]
    outs, padded = refs[-5:-1] if spatial else refs[-2:-1], refs[-1]
    step = pl.program_id(0)

    @pl.when(step == 0)
    def _():
        fill(padded.at[0], mine[...], other[...], spatial)
        fill(padded.at[1], swapped[0][...], swapped[1][...], spatial)
        fill(padded.at[2], pair[...], both[...], spatial)
        fill(padded.at[3], swapped[2][...], swapped[3][...], spatial)

    right = padded[(slice(None),) + tap_rows(spatial, step + first)]
    blocks = jnp.concatenate([ref[...].reshape(-1, 4 * ROWS) for ref in left], axis=0)
    result = contract_inner(blocks, right.reshape(4 * ROWS, 2 * CH))
    result = result.astype(BF)
    if not spatial:
        for block in range(4):
            outs[0][index[block], 0] = result[block * SUB : (block + 1) * SUB]
        return
    for block in range(4):
        for place in range(4):

            @pl.when(index[block] == place)
            def _():
                outs[place][0] = result[block * SUB : (block + 1) * SUB]


def wgrad(spatial, first, taps, index, left, fields, *waits):
    if spatial:
        out_specs = [pl.BlockSpec((1, SUB, 2 * CH), lambda i, ix: (i, 0, 0))] * 4
        out_shape = [jax.ShapeDtypeStruct((taps, SUB, 2 * CH), BF)] * 4
    else:
        out_specs = pl.BlockSpec((4, 1, SUB, 2 * CH), lambda i, ix: (0, i, 0, 0))
        out_shape = jax.ShapeDtypeStruct((4, taps, SUB, 2 * CH), BF)
    return pl.pallas_call(
        lambda *refs: wgrad_body(first, spatial, len(left), len(fields), *refs),
        grid_spec=pltpu.PrefetchScalarGridSpec(
            num_scalar_prefetch=1,
            grid=(taps,),
            in_specs=[whole(f.shape) for f in left + fields]
            + [pl.BlockSpec(memory_space=pl.ANY)] * len(waits),
            out_specs=out_specs,
            scratch_shapes=[pltpu.VMEM((4,) + pad_shape(spatial), BF)],
        ),
        out_shape=out_shape,
        compiler_params=params(),
        cost_estimate=cost(4.7 + 1.25 * taps),
    )(index, *left, *fields, *waits)


def after(value, *others):
    return pl.pallas_call(
        lambda *refs: None,
        in_specs=[pl.BlockSpec(memory_space=pl.ANY)] * (1 + len(others)),
        out_specs=pl.BlockSpec(memory_space=pl.ANY),
        out_shape=jax.ShapeDtypeStruct(value.shape, value.dtype),
        input_output_aliases={0: 0},
        cost_estimate=pl.CostEstimate(flops=0, bytes_accessed=0, transcendentals=0),
    )(value, *others)


def together(*values):
    return pl.pallas_call(
        lambda *refs: None,
        in_specs=[pl.BlockSpec(memory_space=pl.ANY)] * len(values),
        out_specs=[pl.BlockSpec(memory_space=pl.ANY)] * len(values),
        out_shape=[jax.ShapeDtypeStruct(value.shape, value.dtype) for value in values],
        input_output_aliases={i: i for i in range(len(values))},
        cost_estimate=pl.CostEstimate(flops=0, bytes_accessed=0, transcendentals=0),
    )(*values)


def per_group(values):
    return jnp.repeat(jnp.sum(values.reshape(-1, C // G), axis=1), C // G)


def local(
    block_input, spatial_out, cotangent, spatial_kernel, temporal_kernel, norm_gain, norm_bias
):
    dp, mp = lax.axis_index("dp"), lax.axis_index("mp")
    y, pair, core = dp // 4, (dp // 2) % 2, dp % 2
    half, z = mp // 4, mp % 4
    quarter = 2 * pair + core
    y_core_groups = [[4 * a + 2 * p + b for a in range(4) for b in range(2)] for p in range(2)]
    y_groups = [[4 * a + b for a in range(4)] for b in range(4)]
    z_groups = [[0, 1, 2, 3], [4, 5, 6, 7]]

    cot = cotangent.reshape(FR, HT * WD, CH)
    spatial_kernel = spatial_kernel.reshape(9, C, CH)

    def exchange(turned):
        pick = lambda k: lax.dynamic_index_in_dim(turned, quarter ^ k, 0, keepdims=False)
        sent = send(pick(1), to_core), send(pick(2), to_pair), send(pick(3), to_pair_core)
        return pick(0), sent

    def kernel_part(kernel):
        start = (1 - half) * 1024 + y * 256 + core * 128
        return lax.dynamic_slice_in_dim(kernel, start, 128, axis=1)

    tk_part = send(kernel_part(temporal_kernel), to_half)
    own, parts = exchange(spatial_out.reshape(ROWS, CH).T.reshape(4, SUB, ROWS))
    tk_part, *parts = together(tk_part, *parts)
    saved_part = jnp.concatenate([own, *parts], axis=1)
    saved_left = (lax.all_gather(saved_part, "mp", axis=0, axis_index_groups=z_groups),)

    tk_parts = [send(tk_part, to_y(k)) for k in (1, 2, 3)]
    cot_other = send(cot, to_half)
    sk_part = kernel_part(spatial_kernel)
    cot_other, sk_part, *tk_parts = together(cot_other, sk_part, *tk_parts)
    tk_near = jnp.stack([tk_part, *tk_parts])

    flat_in = block_input.reshape(FR, HT * WD, CH).transpose(1, 0, 2).reshape(ROWS, CH).astype(F32)
    count = ROWS * (C // G)
    center = per_group(jnp.sum(flat_in, axis=0)) / count
    spread = per_group(jnp.sum(jnp.square(flat_in - center), axis=0)) / count
    inverse = lax.rsqrt(spread + EPSILON)
    normed_hat = (flat_in - center) * inverse
    normed = normed_hat * norm_gain + norm_bias
    gate = jax.nn.sigmoid(normed)
    hidden = (normed * gate).astype(BF)

    def blocks_of(spatial, steps, *arrays):
        blocks = [(z + k) % 4 for k in steps]
        if spatial:
            near, far = [2 * b for b in blocks], [2 * b + 1 for b in blocks]
        else:
            near = far = [(y - b) % 4 for b in blocks]
        index = [0 if spatial else core] + [half * 4 + b for b in blocks] + near + far
        index = jnp.stack([jnp.int32(i) for i in index])
        kinds = [BF if k else F32 for k in steps]
        return dgrad(spatial, len(steps), kinds, index, *arrays)

    def total_of(mine, sent):
        one, two, three = [v.astype(F32) for v in sent]
        return mine + (one + three) + two

    tk_far = send(tk_near, to_core)
    arrays = (cot, cot_other, temporal_kernel, tk_near, tk_far)
    sk_part = send(after(sk_part, tk_far), to_half)
    up, down, far, mine = blocks_of(False, (1, 3, 2, 0), *arrays)
    sk_part, up, down, far = together(sk_part, up, down, far)
    sk_other = lax.all_gather(sk_part, "dp", axis=0, axis_index_groups=y_core_groups)

    up, down = send(up, to_z(1)), send(down, to_z(3))
    cot_late = after(cot, mine)
    cot_pair, cot_both = send(cot_late, to_pair), send(cot_late, to_both)
    up, down, far, cot_pair, cot_both = together(up, down, far, cot_pair, cot_both)

    own, parts = exchange(after(hidden.T.reshape(4, SUB, ROWS), up))
    cot_near = (cot, cot_other, cot_pair, cot_both)
    cot_swapped = send(jnp.stack(cot_near), to_core)
    far = send(far, to_z(2))
    cot_swapped, *parts, far = together(cot_swapped, *parts, far)
    hidden_part = jnp.concatenate([own, *parts], axis=1)
    hidden_left = (lax.all_gather(hidden_part, "mp", axis=0, axis_index_groups=z_groups),)
    saved_grad = total_of(mine, (up, far, down)).astype(BF)
    saved_grad = saved_grad.reshape(FR, HT * WD, CH).transpose(1, 0, 2).reshape(HT, WD, FR, CH)

    sg_other = send(saved_grad, to_half)
    slots = jnp.array([[0, 2, 1, 3], [2, 0, 3, 1]], jnp.int32)[half]
    fields = cot_near + (cot_swapped,)
    temporal_parts = wgrad(False, 0, 3, slots, saved_left, fields, saved_grad)
    sg_other, temporal_parts = together(sg_other, temporal_parts)
    temporal_total = lax.psum_scatter(
        temporal_parts, "dp", scatter_dimension=0, axis_index_groups=y_groups
    )

    arrays = (saved_grad, sg_other, spatial_kernel, sk_other, sk_other)
    up, down = blocks_of(True, (1, 3), *arrays)
    sg_late = after(saved_grad, up)
    up, down = send(up, to_z(1)), send(down, to_z(3))
    sg_pair, sg_both = send(sg_late, to_pair), send(sg_late, to_both)
    far, mine = blocks_of(True, (2, 0), *arrays, sg_late)
    up, down, far, sg_pair, sg_both = together(up, down, far, sg_pair, sg_both)

    sg_near = (saved_grad, sg_other, sg_pair, sg_both)
    far = send(far, to_z(2))
    sg_fields = sg_near + tuple(send(value, to_core) for value in sg_near)
    parts = wgrad(True, 0, 9, (slots - y) % 4, hidden_left, sg_fields)
    far, *parts = together(far, *parts)
    hidden_grad = total_of(mine, (up, far, down))

    normed_grad = hidden_grad * gate * (1.0 + normed * (1.0 - gate))
    gain_sum = jnp.sum(normed_grad * normed_hat, axis=0)
    bias_sum = jnp.sum(normed_grad, axis=0)
    first = per_group(bias_sum * norm_gain) / count
    second = per_group(gain_sum * norm_gain) / count
    branch = inverse * (normed_grad * norm_gain - first - normed_hat * second)
    branch = branch.reshape(HT * WD, FR, CH).transpose(1, 0, 2)
    input_grad = (cot.astype(F32) + branch).astype(BF).reshape(block_input.shape)

    def to_owners(total):
        total = total.astype(BF)
        mine, other = total[:, :, :CH], total[:, :, CH:]
        same = half == core
        first, second = jnp.where(same, mine, other), jnp.where(same, other, mine)
        first, second = together(first, second)
        return send(first, to_owner(0)), send(second, to_owner(1))

    def owned(first, second):
        low, high = jnp.where(half == 0, first, second), jnp.where(half == 0, second, first)
        return jnp.concatenate([low, high], axis=1).astype(F32)

    sums = lax.all_gather(jnp.stack([gain_sum, bias_sum]), "dp", axis=0)
    others = [send(parts[k], to_y(k)) for k in (1, 2, 3)]
    *others, sums = together(*others, sums)
    total = parts[0].astype(F32)
    for other in others:
        total = total + other.astype(F32)
    temporal_total = after(temporal_total, parts[0])
    grads = owned(*to_owners(jnp.concatenate([total.astype(BF), temporal_total])))
    spatial_grad, temporal_grad = grads[:9].reshape(3, 3, CH // 2, CH), grads[9:]
    sums = jnp.sum(sums, axis=0)
    return (input_grad, spatial_grad, temporal_grad, sums[0], sums[1])


def solution(mesh):
    placed = (
        P("dp", None, None, None, "mp"),
        P("dp", None, None, None, "mp"),
        P("dp", None, None, None, "mp"),
        P(None, None, None, "mp"),
        P(None, None, "mp"),
        P("mp"),
        P("mp"),
    )
    return jax.shard_map(
        local,
        mesh=mesh,
        in_specs=placed,
        out_specs=(
            P("dp", None, None, None, "mp"),
            P(None, None, "dp", "mp"),
            P(None, "dp", "mp"),
            P("mp"),
            P("mp"),
        ),
        check_vma=False,
    )
```
